256 devices in a mesh: seq: 64 (over z, y, core), ch: 4 (over x).
Axes of the slice: x: 4, y: 4, z: 8, core: 2. Of those that a mesh axis runs over, the one named last changes fastest.
Arguments:
- q_feat: bfloat16 [16384, 4096], P('seq', 'ch'), may hold values from -6 to 6
- k_feat: bfloat16 [16384, 4096], P('seq', 'ch'), may hold values from -6 to 6
- v_feat: bfloat16 [16384, 4096], P('seq', 'ch'), may hold values from -6 to 6
- short_taps: float32 [3, 3, 4096], P(None, None, 'ch'), may hold values from -3.5 to 3.5
- decay_rate: float32 [16, 4096], P(None, 'ch'), may hold values from 0 to 1, as said below
- residue: float32 [16, 4096], P(None, 'ch'), may hold values from -1 to 1
- skip_gain: float32 [4096], P('ch'), may hold values from -6 to 6
- out_weight: bfloat16 [4096, 4096], P('seq', 'ch'), may hold values from -0.09375 to 0.09375
- doc_starts: int32 [64, 4], P('seq'), may hold values from 0 to 256, as said below
- reset_flags: int32 [64, 4], P('seq'), may hold values from 0 to 1, as said below
Outputs:
- mixer_out: bfloat16 [16384, 4096], P('seq', 'ch')
The draws below stay inside these ranges and needn't reach their ends.
Inputs may be any that keep to these rules, and one draw needn't show every extreme that they name: `doc_starts`: row s lists ascending the offsets within shard s at which documents begin, then unused slots holding 256; a shard holds at most 4 starts, some shard exactly 4, some shard none. `reset_flags`: only used slots hold 1; in each shard at most one slot holds 1, and some shard has one. `decay_rate`: positive rates.
All inputs are finite; a program needn't handle non-finite values.
Results may differ from the reference program's by a relative error of at most 0.018.
Values may be sent and summed in bfloat16 or wider, within the bound.
No kernel may reach another device: no remote copies, remote signals or barrier semaphores. Data moves between devices by JAX's collectives and lax.ppermute only.
A program may use at most 128 MiB of HBM per device.

```python
import jax
import jax.numpy as jnp
from jax import lax

D = 4096
MODES = 16
SHORT = 3
BLOCK = 128
SLOTS = 4
TOK = 256
SHARDS = 64
SEQLEN = 16384
GROUP = 1024
N_CH = 4


def rate_table(key):
    picker = jax.random.uniform(jax.random.fold_in(key, 11), (MODES, D))
    fast_rate = jnp.exp(jax.random.uniform(jax.random.fold_in(key, 12), (MODES, D), minval=jnp.log(1.0 / 50.0), maxval=jnp.log(1.0 / 30.0)))
    middle_rate = jnp.exp(jax.random.uniform(jax.random.fold_in(key, 14), (MODES, D), minval=jnp.log(0.25), maxval=jnp.log(2.5))) / TOK
    slow_rate = jnp.exp(jax.random.uniform(jax.random.fold_in(key, 13), (MODES, D), minval=jnp.log(0.1), maxval=jnp.log(2.0))) / SEQLEN
    fast_share = 0.3
    middle_share = 0.3
    chosen = jnp.where(picker < fast_share, fast_rate, jnp.where(picker < fast_share + middle_share, middle_rate, slow_rate))
    return chosen.astype(jnp.float32)


def draw_decay_rate(key, part):
    return rate_table(key)


def draw_residue(key, part):
    rates = rate_table(key)
    base = jnp.clip(jax.random.normal(jax.random.fold_in(key, 22), (MODES, D)), -4.0, 4.0)
    return (0.35 * base * jnp.sqrt(-jnp.expm1(-2.0 * rates))).astype(jnp.float32)


def shard_layout(key):
    base = jax.random.fold_in(key, 7)
    shard_ids = jnp.arange(SHARDS, dtype=jnp.int32)
    full_shard = jax.random.randint(jax.random.fold_in(base, 1), (), 0, SHARDS)
    counts = jax.random.randint(jax.random.fold_in(base, 2), (SHARDS,), 0, SLOTS + 1)
    counts = jnp.where(shard_ids == full_shard, SLOTS, counts)
    counts = jnp.where(shard_ids == (full_shard + 1) % SHARDS, 0, counts)
    scores = jax.random.randint(jax.random.fold_in(base, 3), (SHARDS, TOK), 0, 65536) * TOK + jnp.arange(TOK, dtype=jnp.int32)[None, :]
    _, chosen = lax.top_k(scores, SLOTS)
    chosen = jnp.sort(chosen, axis=1)
    slot_ids = jnp.arange(SLOTS, dtype=jnp.int32)[None, :]
    used_slot = slot_ids < counts[:, None]
    starts = jnp.where(used_slot, chosen, TOK).astype(jnp.int32)
    picked = jax.random.randint(jax.random.fold_in(base, 4), (SHARDS,), 0, 65536) % jnp.maximum(counts, 1)
    coins = (jax.random.randint(jax.random.fold_in(base, 5), (SHARDS,), 0, 16) == 0) | (shard_ids == full_shard)
    flags = ((slot_ids == picked[:, None]) & used_slot & coins[:, None]).astype(jnp.int32)
    return (starts, flags)


def draw_doc_starts(key, part):
    return shard_layout(key)[0]


def draw_reset_flags(key, part):
    return shard_layout(key)[1]


def shard_levels(stream_key, dims, split, least, largest):
    level = 1.0
    for axis_at, shards_of in split:
        steps = jax.random.uniform(jax.random.fold_in(jax.random.fold_in(stream_key, 6), axis_at), (shards_of,), jnp.float32, least / len(split), largest / len(split))
        level = level * jnp.repeat(jnp.exp(steps), dims[axis_at] // shards_of).reshape((-1,) + (1,) * (len(dims) - 1 - axis_at))
    return level


def gaussian(stream_key, dims, width, limit, split=(), kind=jnp.bfloat16):
    gain = shard_levels(stream_key, dims, split, -0.22, 0.18) if split else 1.0
    array = jax.random.normal(stream_key, dims, jnp.float32) * width * gain
    return jnp.minimum(jnp.maximum(array, -limit), limit).astype(kind)


def setup_inputs(seed: int = 0) -> dict:
    key_of = jax.random.split(jax.random.key(seed), 11)
    return {
        "q_feat": gaussian(key_of[0], (SEQLEN, D), 1.0, 6.0, ((0, 64), (1, 4))),
        "k_feat": gaussian(key_of[1], (SEQLEN, D), 1.0, 6.0, ((0, 64), (1, 4))),
        "v_feat": gaussian(key_of[2], (SEQLEN, D), 1.0, 6.0, ((0, 64), (1, 4))),
        "short_taps": gaussian(key_of[3], (3, SHORT, D), 0.6, 3.5, ((2, 4),), jnp.float32),
        "decay_rate": draw_decay_rate(jax.random.fold_in(key_of[10], 71), 0),
        "residue": draw_residue(jax.random.fold_in(key_of[10], 71), 0),
        "skip_gain": gaussian(key_of[6], (D,), 1.0, 6.0, ((0, 4),), jnp.float32),
        "out_weight": gaussian(key_of[7], (D, D), D ** -0.5, 0.09375, ((0, 64), (1, 4))),
        "doc_starts": draw_doc_starts(jax.random.fold_in(key_of[10], 71), 0),
        "reset_flags": draw_reset_flags(jax.random.fold_in(key_of[10], 71), 0),
    }


def short_filter(features, rim_rows, tap_weights, keep_mask):
    token_rows = features.shape[0]
    tap_count = tap_weights.shape[0]
    joined = jnp.concatenate([rim_rows, features], axis=0)
    summed = tap_weights[0] * features.astype(jnp.float32)
    valid_mask = jnp.ones((token_rows,), jnp.float32)
    for offset in range(1, tap_count):
        valid_mask = valid_mask * jnp.concatenate([jnp.ones((offset - 1,), jnp.float32), keep_mask[:token_rows - offset + 1]])
        lagged = joined[tap_count - 1 - offset:tap_count - 1 - offset + token_rows].astype(jnp.float32)
        summed = summed + tap_weights[offset] * valid_mask[:, None] * lagged
    return summed.astype(jnp.bfloat16)


def document_marks(doc_starts, reset_flags):
    shard_base = (jnp.arange(SHARDS, dtype=jnp.int32) * TOK)[:, None]
    used_slot = doc_starts < TOK
    spots = jnp.where(used_slot, shard_base + doc_starts, SEQLEN).reshape(-1).astype(jnp.int32)
    flagged = ((reset_flags == 1) & used_slot).astype(jnp.float32).reshape(-1)
    starts_at = jnp.zeros((SEQLEN + 1,), jnp.float32).at[spots].max(jnp.ones_like(flagged))[:SEQLEN]
    resets = jnp.zeros((SEQLEN + 1,), jnp.float32).at[spots].max(flagged)[:SEQLEN]
    return starts_at, resets


def modal_filter(gated, resets, decay_rate, residue):
    highest = lax.Precision.HIGHEST
    decay_factor = jnp.exp(-decay_rate)
    steps_axis = jnp.arange(1, BLOCK + 1, dtype=jnp.float32)
    weighted = jnp.exp(-steps_axis[:, None, None] * decay_rate[None]) * residue[None]
    block_pow = jnp.exp(-BLOCK * decay_rate)
    gated_blocks = gated.reshape(SEQLEN // BLOCK, BLOCK, D)
    reset_blocks = resets.reshape(SEQLEN // BLOCK, BLOCK)

    def row_step(carried_state, row_item):
        gated_row, reset_row = row_item
        carried_state = decay_factor * carried_state * (1.0 - reset_row) + gated_row[None, :]
        return carried_state, jnp.sum(residue * carried_state, axis=0)

    def block_step(carried_state, block_item):
        gated_block, reset_block = block_item
        local_end, local_out = lax.scan(row_step, jnp.zeros((MODES, D), jnp.float32), (gated_block, reset_block))
        alive_mask = jnp.cumprod(1.0 - reset_block)
        carried = jnp.einsum("bnc,nc->bc", weighted, carried_state, precision=highest) * alive_mask[:, None]
        next_state = local_end + block_pow * carried_state * alive_mask[-1]
        return next_state, local_out + carried

    _, outputs = lax.scan(block_step, jnp.zeros((MODES, D), jnp.float32), (gated_blocks, reset_blocks))
    return outputs.reshape(SEQLEN, D)


def reference(q_feat, k_feat, v_feat, short_taps, decay_rate, residue, skip_gain, out_weight, doc_starts, reset_flags):
    starts_at, resets = document_marks(doc_starts, reset_flags)
    keep_mask = 1.0 - starts_at
    empty_rim = jnp.zeros((SHORT - 1, D), jnp.bfloat16)
    q_short = short_filter(q_feat, empty_rim, short_taps[0], keep_mask)
    k_short = short_filter(k_feat, empty_rim, short_taps[1], keep_mask)
    v_short = short_filter(v_feat, empty_rim, short_taps[2], keep_mask)
    gated = k_short.astype(jnp.float32) * v_short.astype(jnp.float32)
    filtered = modal_filter(gated, resets, decay_rate, residue)
    mixed = (q_short.astype(jnp.float32) * (filtered + skip_gain[None, :] * gated)).astype(jnp.bfloat16)

    def project_rows(row_block):
        summed = jnp.zeros((TOK, D), jnp.float32)
        for group_index in range(N_CH):
            first = group_index * GROUP
            group_term = jnp.dot(row_block[:, first:first + GROUP], out_weight[:, first:first + GROUP].T, preferred_element_type=jnp.float32)
            rounded = lax.optimization_barrier(group_term.astype(jnp.bfloat16))
            summed = summed + rounded.astype(jnp.float32)
        return summed.astype(jnp.bfloat16)

    projected = lax.map(project_rows, mixed.reshape(SHARDS, TOK, D))
    return projected.reshape(SEQLEN, D)
```

```python
import jax
import jax.numpy as jnp
from jax import lax
from jax.experimental import pallas as pl
from jax.experimental.pallas import tpu as pltpu
from jax.sharding import PartitionSpec as P

MODES = 16
ROWS = 256
LANES = 128
GROUPS = 8
STEPS = 8
CHUNKS = ROWS // STEPS
PIECE = 64


def cyclic(block, shift):
    count = lax.axis_size("seq")
    return lax.ppermute(block, "seq", [(i, shift(i)) for i in range(count)])


def reset_place(starts_ref, flags_ref):
    place = jnp.int32(0)
    found = jnp.int32(0)
    for slot in range(4):
        hit = (flags_ref[0, slot] == 1) & (starts_ref[0, slot] < ROWS)
        place = jnp.where(hit, starts_ref[0, slot], place)
        found = jnp.where(hit, jnp.int32(1), found)
    return place, found


def row_slice(t):
    return pl.ds(pl.multiple_of(t * GROUPS, GROUPS), GROUPS)


def front_kernel(starts_ref, flags_ref, q_ref, k_ref, v_ref, halo_ref, taps_ref, rate_ref,
                 q_out, gated_out, state_out, wide):
    for feature, source in enumerate((k_ref, v_ref, q_ref)):
        which = (1, 2, 0)[feature]
        wide[feature, 8:, :] = source[...].astype(jnp.float32)
        wide[feature, 6:8, :] = halo_ref[2 * which : 2 * which + 2, :].astype(jnp.float32)
    for first in range(0, ROWS, PIECE):
        t = lax.broadcasted_iota(jnp.int32, (PIECE, LANES), 0) + first
        keep_one = jnp.ones((PIECE, LANES), jnp.float32)
        keep_two = keep_one
        for slot in range(4):
            at = starts_ref[0, slot]
            keep_one = jnp.where(t == at, 0.0, keep_one)
            keep_two = jnp.where((t == at) | (t == at + 1), 0.0, keep_two)
        for group in range(GROUPS):
            lanes = slice(group * LANES, (group + 1) * LANES)

            def short(feature, which):
                total = taps_ref[3 * which : 3 * which + 1, lanes] * wide[
                    feature, 8 + first : 8 + first + PIECE, lanes]
                total = total + (taps_ref[3 * which + 1 : 3 * which + 2, lanes] * keep_one) * wide[
                    feature, 7 + first : 7 + first + PIECE, lanes]
                total = total + (taps_ref[3 * which + 2 : 3 * which + 3, lanes] * keep_two) * wide[
                    feature, 6 + first : 6 + first + PIECE, lanes]
                return total.astype(jnp.bfloat16).astype(jnp.float32)

            rows = pl.ds(first * GROUPS + group, PIECE, stride=GROUPS)
            gated_out[rows, :] = short(0, 1) * short(1, 2)
            q_out[rows, :] = short(2, 0)
    place, found = reset_place(starts_ref, flags_ref)
    decay = [jnp.exp(-rate_ref[n * GROUPS : (n + 1) * GROUPS, :]) for n in range(MODES)]

    def chunk(index, state):
        for step in range(STEPS):
            t = index * STEPS + step
            row = jnp.where(t >= place, gated_out[row_slice(t), :], 0.0)
            state = tuple(decay[n] * state[n] + row for n in range(MODES))
        return state

    zero = jnp.zeros((GROUPS, LANES), jnp.float32)
    state = lax.fori_loop(place // STEPS, CHUNKS, chunk, (zero,) * MODES)
    for n in range(MODES):
        state_out[n * GROUPS : (n + 1) * GROUPS, :] = state[n]
    state_out[MODES * GROUPS :, :] = jnp.full((GROUPS, LANES), 1 - found, jnp.int32).astype(jnp.float32)


def inner_kernel(starts_ref, flags_ref, gated_ref, rate_ref, residue_ref, skip_ref, out_ref):
    place, found = reset_place(starts_ref, flags_ref)
    decay = [jnp.exp(-rate_ref[n * GROUPS : (n + 1) * GROUPS, :]) for n in range(MODES)]
    weight = [residue_ref[n * GROUPS : (n + 1) * GROUPS, :] for n in range(MODES)]
    skip = skip_ref[...]
    cut_chunk = jnp.where(found == 1, place // STEPS, CHUNKS)

    def run(index, state, cutting):
        for step in range(STEPS):
            t = index * STEPS + step
            row = gated_ref[row_slice(t), :]
            if cutting:
                state = tuple(jnp.where(t == place, 0.0, state[n]) for n in range(MODES))
            state = tuple(decay[n] * state[n] + row for n in range(MODES))
            terms = [weight[n] * state[n] for n in range(MODES)] + [skip * row]
            while len(terms) > 1:
                paired = [terms[i] + terms[i + 1] for i in range(0, len(terms) - 1, 2)]
                terms = paired + terms[len(terms) - len(terms) % 2 :]
            out_ref[row_slice(t), :] = terms[0]
        return state

    zero = jnp.zeros((GROUPS, LANES), jnp.float32)
    state = (zero,) * MODES
    state = lax.fori_loop(0, cut_chunk, lambda i, s: run(i, s, False), state)
    state = lax.fori_loop(
        cut_chunk, jnp.minimum(cut_chunk + 1, CHUNKS), lambda i, s: run(i, s, True), state)
    lax.fori_loop(cut_chunk + 1, CHUNKS, lambda i, s: run(i, s, False), state)


def mix_kernel(starts_ref, flags_ref, entering_ref, rate_ref, residue_ref, q_ref, inner_ref,
               mixed_out, rows_ref):
    place, found = reset_place(starts_ref, flags_ref)
    limit = jnp.where(found == 1, place, ROWS)
    decay = [jnp.exp(-rate_ref[n * GROUPS : (n + 1) * GROUPS, :]) for n in range(MODES)]
    carried = tuple(
        residue_ref[n * GROUPS : (n + 1) * GROUPS, :] * entering_ref[n * GROUPS : (n + 1) * GROUPS, :]
        for n in range(MODES))
    live_chunks = (limit + STEPS - 1) // STEPS

    def live(index, carried):
        for step in range(STEPS):
            t = index * STEPS + step
            carried = tuple(decay[n] * carried[n] for n in range(MODES))
            terms = list(carried)
            while len(terms) > 1:
                terms = [terms[i] + terms[i + 1] for i in range(0, len(terms), 2)]
            from_before = jnp.where(t < limit, terms[0], 0.0)
            rows_ref[row_slice(t), :] = q_ref[row_slice(t), :] * (inner_ref[row_slice(t), :] + from_before)
        return carried

    def rest(index, _):
        for step in range(STEPS):
            t = index * STEPS + step
            rows_ref[row_slice(t), :] = q_ref[row_slice(t), :] * inner_ref[row_slice(t), :]
        return 0

    lax.fori_loop(0, live_chunks, live, carried)
    lax.fori_loop(live_chunks, CHUNKS, rest, 0)
    for group in range(GROUPS):
        mixed_out[:, group * LANES : (group + 1) * LANES] = rows_ref[
            pl.ds(group, ROWS, stride=GROUPS), :].astype(jnp.bfloat16)


SMALL = pl.BlockSpec(memory_space=pltpu.SMEM)
WHOLE = pl.BlockSpec(memory_space=pltpu.VMEM)
LIMIT = 32 * 1024 * 1024


def call(kernel, outs, count, scratch=(), flops=0, moved=0):
    return pl.pallas_call(
        kernel,
        out_shape=outs,
        in_specs=[SMALL] * 2 + [WHOLE] * count,
        out_specs=jax.tree.map(lambda _: WHOLE, outs),
        scratch_shapes=scratch,
        compiler_params=pltpu.CompilerParams(vmem_limit_bytes=LIMIT),
        cost_estimate=pl.CostEstimate(flops=flops, bytes_accessed=moved, transcendentals=0),
    )


def f32(*shape):
    return jax.ShapeDtypeStruct(shape, jnp.float32)


STATE = MODES * GROUPS


def digit_round(message, pass_factor, digit, stride, last):
    def back(k):
        def target(i):
            d = (i // stride) % 4
            return i - d * stride + ((d + k) % 4) * stride
        return target

    count = lax.axis_size("seq")
    if last:
        got = {
            k: lax.ppermute(message, "seq", [(i, i + k * stride) for i in range(count - k * stride)])
            for k in (3, 2, 1)
        }
    else:
        got = {k: cyclic(message, back(k)) for k in (3, 2, 1)}
    mine = (lax.axis_index("seq") // stride) % 4

    def join(total, later):
        return later[:STATE] + pass_factor * later[STATE, 0] * total

    entering = jnp.zeros((STATE, LANES), jnp.float32)
    alive = jnp.float32(1)
    for k in (3, 2, 1):
        entering = jnp.where(k <= mine, join(entering, got[k]), 0.0)
        alive = alive * jnp.where(k <= mine, got[k][STATE, 0], 1.0)
    if last:
        return entering, alive, None
    total = join(entering, message)
    whole_alive = message[STATE, 0]
    for k in (3, 2, 1):
        total = jnp.where(k > mine, join(total, got[k]), total)
        whole_alive = whole_alive * got[k][STATE, 0]
    following = jnp.concatenate(
        [total, jnp.full((GROUPS, LANES), 1.0, jnp.float32) * whole_alive], axis=0)
    return entering, alive, following


def local(q_feat, k_feat, v_feat, short_taps, decay_rate, residue, skip_gain, out_weight,
          doc_starts, reset_flags):
    weight = lax.all_gather(out_weight, "seq", axis=0, tiled=True)
    ends = jnp.any(doc_starts[0] == ROWS - 1)
    scale = jnp.stack([jnp.where(ends, 0.0, 1.0), jnp.float32(1)]).astype(jnp.bfloat16)
    tails = jnp.concatenate(
        [part[ROWS - 2 :] * scale[:, None] for part in (q_feat, k_feat, v_feat)], axis=0)
    count = lax.axis_size("seq")
    halo = lax.ppermute(tails, "seq", [(i, i + 1) for i in range(count - 1)])
    rate = decay_rate.reshape(STATE, LANES)
    gain = residue.reshape(STATE, LANES)
    skip = skip_gain.reshape(GROUPS, LANES)
    taps = short_taps.reshape(9, GROUPS * LANES)
    q_rows, gated, message = call(
        front_kernel,
        (f32(ROWS * GROUPS, LANES), f32(ROWS * GROUPS, LANES), f32(STATE + GROUPS, LANES)),
        6,
        scratch=[pltpu.VMEM((3, ROWS + 8, GROUPS * LANES), jnp.float32)],
        flops=20_000_000,
        moved=4_000_000,
    )(doc_starts, reset_flags, q_feat, k_feat, v_feat, halo, taps, rate)
    inner = call(inner_kernel, f32(ROWS * GROUPS, LANES), 4, flops=20_000_000, moved=4_000_000)(
        doc_starts, reset_flags, gated, rate, gain, skip)
    seq = lax.axis_index("seq")
    enter_low, alive_low, next_message = digit_round(message, jnp.exp(-256.0 * rate), 0, 1, False)
    enter_mid, alive_mid, next_message = digit_round(
        next_message, jnp.exp(-1024.0 * rate), 1, 4, False)
    enter_high, _, _ = digit_round(next_message, jnp.exp(-4096.0 * rate), 2, 16, True)
    low = (seq % 4).astype(jnp.float32)
    mid = ((seq // 4) % 4).astype(jnp.float32)
    entering = enter_mid + jnp.exp(-1024.0 * mid * rate) * alive_mid * enter_high
    entering = enter_low + jnp.exp(-256.0 * low * rate) * alive_low * entering
    mixed = call(
        mix_kernel,
        jax.ShapeDtypeStruct((ROWS, GROUPS * LANES), jnp.bfloat16),
        5,
        scratch=[pltpu.VMEM((ROWS * GROUPS, LANES), jnp.float32)],
        flops=20_000_000,
        moved=4_000_000,
    )(doc_starts, reset_flags, entering, rate, gain, q_rows, inner)
    projected = lax.dot_general(
        mixed, weight, (((1,), (1,)), ((), ())), preferred_element_type=jnp.float32)
    return lax.psum_scatter(projected.astype(jnp.bfloat16), "ch", scatter_dimension=1, tiled=True)


def solution(mesh):
    placed = (
        P("seq", "ch"),
        P("seq", "ch"),
        P("seq", "ch"),
        P(None, None, "ch"),
        P(None, "ch"),
        P(None, "ch"),
        P("ch"),
        P("seq", "ch"),
        P("seq", None),
        P("seq", None),
    )
    return jax.shard_map(
        local, mesh=mesh, in_specs=placed, out_specs=P("seq", "ch"), check_vma=False
    )
```

```python
import jax
import jax.numpy as jnp
from jax import lax
from jax.experimental import pallas as pl
from jax.experimental.pallas import tpu as pltpu
from jax.sharding import PartitionSpec as P

MODES = 16
ROWS = 256
LANES = 128
GROUPS = 8
WIDTH = GROUPS * LANES
STEPS = 8
CHUNKS = ROWS // STEPS
PIECE = 64
STATE = MODES * GROUPS
SHARD = 64
HALF = WIDTH // 2
QUARTER = WIDTH // 4


def reset_place(starts_ref, flags_ref):
    place = jnp.int32(0)
    found = jnp.int32(0)
    for slot in range(4):
        hit = (flags_ref[0, slot] == 1) & (starts_ref[0, slot] < ROWS)
        place = jnp.where(hit, starts_ref[0, slot], place)
        found = jnp.where(hit, jnp.int32(1), found)
    return place, found


def row_slice(t):
    return pl.ds(pl.multiple_of(t * GROUPS, GROUPS), GROUPS)


def spread(source, scratch):
    for group in range(GROUPS):
        scratch[pl.ds(group, MODES, stride=GROUPS), :] = source[:, group * LANES : (group + 1) * LANES]


def poles(ref):
    return [ref[n * GROUPS : (n + 1) * GROUPS, :] for n in range(MODES)]


def tail_kernel(starts_ref, q_ref, k_ref, v_ref, shard_ref, out_ref, shard_out):
    ends = starts_ref[0, 0] == ROWS - 1
    for slot in range(1, 4):
        ends = ends | (starts_ref[0, slot] == ROWS - 1)
    scale = jnp.where(ends, 0.0, 1.0)
    for which, source in enumerate((q_ref, k_ref, v_ref)):
        rows = source[...].astype(jnp.float32)
        out_ref[2 * which : 2 * which + 1, :] = rows[14:15, :] * scale
        out_ref[2 * which + 1 : 2 * which + 2, :] = rows[15:16, :]
    out_ref[6:8, :] = jnp.zeros((2, WIDTH), jnp.float32)
    shard_out[...] = shard_ref[...]


def column_kernel(shard_ref, far_ref, halo_ref, out_ref):
    del halo_ref
    out_ref[:SHARD, :] = shard_ref[...]
    out_ref[SHARD:, :] = far_ref[...]


def front_kernel(starts_ref, flags_ref, q_hbm, k_hbm, v_hbm, halo_ref, taps_ref, rate_ref,
                 q_out, gated_out, state_out, held, wide, spread_rate, sems):
    copies = [
        pltpu.make_async_copy(source, held.at[feature], sems.at[feature])
        for feature, source in enumerate((k_hbm, v_hbm, q_hbm))
    ]
    for copy in copies:
        copy.start()
    spread(rate_ref, spread_rate)
    for feature in range(3):
        which = (1, 2, 0)[feature]
        wide[feature, 6:8, :] = halo_ref[2 * which : 2 * which + 2, :]
        copies[feature].wait()
        wide[feature, 8:, :] = held[feature].astype(jnp.float32)
    for first in range(0, ROWS, PIECE):
        t = lax.broadcasted_iota(jnp.int32, (PIECE, LANES), 0) + first
        keep_one = jnp.ones((PIECE, LANES), jnp.float32)
        keep_two = keep_one
        for slot in range(4):
            at = starts_ref[0, slot]
            keep_one = jnp.where(t == at, 0.0, keep_one)
            keep_two = jnp.where((t == at) | (t == at + 1), 0.0, keep_two)
        for group in range(GROUPS):
            lanes = slice(group * LANES, (group + 1) * LANES)

            def short(feature, which):
                total = taps_ref[which, 0:1, lanes] * wide[feature, 8 + first : 8 + first + PIECE, lanes]
                total = total + (taps_ref[which, 1:2, lanes] * keep_one) * wide[
                    feature, 7 + first : 7 + first + PIECE, lanes]
                total = total + (taps_ref[which, 2:3, lanes] * keep_two) * wide[
                    feature, 6 + first : 6 + first + PIECE, lanes]
                return total.astype(jnp.bfloat16).astype(jnp.float32)

            rows = pl.ds(first * GROUPS + group, PIECE, stride=GROUPS)
            gated_out[rows, :] = short(0, 1) * short(1, 2)
            q_out[rows, :] = short(2, 0)
    place, found = reset_place(starts_ref, flags_ref)
    decay = [jnp.exp(-rate) for rate in poles(spread_rate)]

    def chunk(index, state):
        for step in range(STEPS):
            t = index * STEPS + step
            row = jnp.where(t >= place, gated_out[row_slice(t), :], 0.0)
            state = tuple(decay[n] * state[n] + row for n in range(MODES))
        return state

    zero = jnp.zeros((GROUPS, LANES), jnp.float32)
    state = lax.fori_loop(place // STEPS, CHUNKS, chunk, (zero,) * MODES)
    for n in range(MODES):
        state_out[n * GROUPS : (n + 1) * GROUPS, :] = state[n]
    state_out[STATE:, :] = jnp.full((GROUPS, LANES), 1 - found, jnp.int32).astype(jnp.float32)


def digit_join(mine, got, length, spread_rate, total=None, own=None):
    entering, whole = [], []
    alive = jnp.ones((GROUPS, LANES), jnp.float32)
    whole_alive = alive
    flags = [ref[STATE:, :] for ref in got]
    for k, flag in zip((3, 2, 1), flags):
        alive = alive * jnp.where(k <= mine, flag, 1.0)
    for n in range(MODES):
        rows = slice(n * GROUPS, (n + 1) * GROUPS)
        passing = jnp.exp(-length * spread_rate[rows, :])
        value = jnp.zeros((GROUPS, LANES), jnp.float32)
        for k, ref, flag in zip((3, 2, 1), got, flags):
            value = jnp.where(k <= mine, ref[rows, :] + passing * flag * value, 0.0)
        entering.append(value)
        if own is not None:
            value = own[rows, :] + passing * own[STATE:, :] * value
            for k, ref, flag in zip((3, 2, 1), got, flags):
                value = jnp.where(k > mine, ref[rows, :] + passing * flag * value, value)
            whole.append(value)
    if own is not None:
        whole_alive = own[STATE:, :] * flags[0] * flags[1] * flags[2]
    return entering, alive, whole, whole_alive


def low_kernel(own, got3, got2, got1, rate_ref, enter_out, next_out, spread_rate):
    spread(rate_ref, spread_rate)
    mine = lax.axis_index("seq") % 4
    entering, alive, whole, whole_alive = digit_join(
        mine, (got3, got2, got1), 256.0, spread_rate, own=own)
    for n in range(MODES):
        enter_out[n * GROUPS : (n + 1) * GROUPS, :] = entering[n]
        next_out[n * GROUPS : (n + 1) * GROUPS, :] = whole[n]
    enter_out[STATE:, :] = alive
    next_out[STATE:, :] = whole_alive


def middle_kernel(own, got3, got2, got1, low, rate_ref, enter_out, next_out, spread_rate):
    spread(rate_ref, spread_rate)
    seq = lax.axis_index("seq")
    entering, alive, whole, whole_alive = digit_join(
        (seq // 4) % 4, (got3, got2, got1), 1024.0, spread_rate, own=own)
    span = (seq % 4).astype(jnp.float32) * 256.0
    low_alive = low[STATE:, :]
    for n in range(MODES):
        rows = slice(n * GROUPS, (n + 1) * GROUPS)
        reach = jnp.exp(-span * spread_rate[rows, :]) * low_alive
        enter_out[rows, :] = low[rows, :] + reach * entering[n]
        next_out[rows, :] = whole[n]
    enter_out[STATE:, :] = alive * low_alive
    next_out[STATE:, :] = whole_alive


def mix_kernel(starts_ref, flags_ref, got3, got2, got1, before, rate_ref, residue_ref, skip_ref,
               q_ref, gated_ref, mixed_out, spread_rate, spread_gain, rows_ref):
    spread(rate_ref, spread_rate)
    spread(residue_ref, spread_gain)
    skip = jnp.concatenate(
        [skip_ref[:, group * LANES : (group + 1) * LANES] for group in range(GROUPS)], axis=0)
    seq = lax.axis_index("seq")
    entering, _, _, _ = digit_join(seq // 16, (got3, got2, got1), 4096.0, spread_rate)
    span = (seq % 16).astype(jnp.float32) * 256.0
    before_alive = before[STATE:, :]
    state, decay = [], []
    for n, rate in enumerate(poles(spread_rate)):
        rows = slice(n * GROUPS, (n + 1) * GROUPS)
        state.append(before[rows, :] + jnp.exp(-span * rate) * before_alive * entering[n])
        decay.append(jnp.exp(-rate))
    state = tuple(state)
    weight = poles(spread_gain)
    place, found = reset_place(starts_ref, flags_ref)
    cut_chunk = jnp.where(found == 1, place // STEPS, CHUNKS)

    def run(index, state, cutting):
        for step in range(STEPS):
            t = index * STEPS + step
            row = gated_ref[row_slice(t), :]
            if cutting:
                state = tuple(jnp.where(t == place, 0.0, state[n]) for n in range(MODES))
            state = tuple(decay[n] * state[n] + row for n in range(MODES))
            terms = [weight[n] * state[n] for n in range(MODES)] + [skip * row]
            while len(terms) > 1:
                paired = [terms[i] + terms[i + 1] for i in range(0, len(terms) - 1, 2)]
                terms = paired + terms[len(terms) - len(terms) % 2 :]
            rows_ref[row_slice(t), :] = q_ref[row_slice(t), :] * terms[0]
        return state

    state = lax.fori_loop(0, cut_chunk, lambda i, s: run(i, s, False), state)
    state = lax.fori_loop(
        cut_chunk, jnp.minimum(cut_chunk + 1, CHUNKS), lambda i, s: run(i, s, True), state)
    lax.fori_loop(cut_chunk + 1, CHUNKS, lambda i, s: run(i, s, False), state)
    for group in range(GROUPS):
        mixed_out[:, group * LANES : (group + 1) * LANES] = rows_ref[
            pl.ds(group, ROWS, stride=GROUPS), :].astype(jnp.bfloat16)


def project_kernel(turns, mixed_ref, gathered, other, earlier, before, *refs):
    del earlier, before
    outs, weight = refs[: 2 * len(turns)], refs[2 * len(turns)]
    seq, ch = lax.axis_index("seq"), lax.axis_index("ch")
    z, y, core = seq // 8, (seq // 2) % 4, seq % 2
    for slot, turn in enumerate(turns):
        target = (ch + turn) % 4
        for side, source in enumerate((gathered, other)):
            at_core = (core + side) % 2
            for half in range(2):
                age = (z - 2 * target - half + 16) % 8
                for gap in range(2):
                    at_y = (y // 2 + gap) % 2
                    row = pl.multiple_of(((half * 2 + at_y) * 2 + at_core) * SHARD, SHARD)
                    start = pl.multiple_of((age * 2 + gap) * SHARD, SHARD)
                    weight[slot, pl.ds(row, SHARD), :] = source[pl.ds(start, SHARD), :]
        for part in range(2):
            outs[2 * slot + part][...] = lax.dot_general(
                mixed_ref[...], weight[slot, part * QUARTER : (part + 1) * QUARTER, :],
                (((1,), (1,)), ((), ())), preferred_element_type=jnp.float32).astype(jnp.bfloat16)


def add_kernel(right_ref, right_own, left_ref, left_own, right_out, left_out):
    right_out[...] = (right_ref[...].astype(jnp.float32) + right_own[...].astype(jnp.float32)).astype(jnp.bfloat16)
    left_out[...] = (left_ref[...].astype(jnp.float32) + left_own[...].astype(jnp.float32)).astype(jnp.bfloat16)


def summed(own_a, own_b, sum_a, sum_b, one_a, one_b, part):
    chosen = ((own_a, sum_a, one_a), (own_b, sum_b, one_b))[part]
    first, second, third = [ref[...].astype(jnp.float32) for ref in chosen]
    return (first + second + third).astype(jnp.bfloat16)


def total_kernel(*refs):
    for part in range(2):
        refs[6][:, part * QUARTER : (part + 1) * QUARTER] = summed(*refs[:6], part)


def last_kernel(*refs):
    mate, out_ref = refs[6], refs[7]
    parity = (lax.axis_index("seq") // 2) % 2
    for part in range(2):
        mine = summed(*refs[:6], part)
        for at_y in range(2):
            block = 4 * part + 2 * at_y
            lanes = slice(at_y * LANES, (at_y + 1) * LANES)
            out_ref[:, pl.ds(pl.multiple_of((block + parity) * LANES, LANES), LANES)] = mine[:, lanes]
            lanes = slice((2 * part + at_y) * LANES, (2 * part + at_y + 1) * LANES)
            out_ref[:, pl.ds(pl.multiple_of((block + 1 - parity) * LANES, LANES), LANES)] = mate[:, lanes]


SMALL = pl.BlockSpec(memory_space=pltpu.SMEM)
WHOLE = pl.BlockSpec(memory_space=pltpu.VMEM)
FAR = pl.BlockSpec(memory_space=pl.ANY)
LIMIT = 40 * 1024 * 1024


def call(kernel, outs, specs, scratch=(), flops=4_000_000, moved=2_000_000):
    return pl.pallas_call(
        kernel,
        out_shape=outs,
        in_specs=specs,
        out_specs=jax.tree.map(lambda _: WHOLE, outs),
        scratch_shapes=scratch,
        compiler_params=pltpu.CompilerParams(vmem_limit_bytes=LIMIT),
        cost_estimate=pl.CostEstimate(flops=flops, bytes_accessed=moved, transcendentals=0),
    )


def f32(*shape):
    return jax.ShapeDtypeStruct(shape, jnp.float32)


def b16(*shape):
    return jax.ShapeDtypeStruct(shape, jnp.bfloat16)


def move(block, target):
    count = lax.axis_size("seq")
    return lax.ppermute(block, "seq", [(i, target(i)) for i in range(count)])


def along_y(block, gap):
    return move(block, lambda i: (i // 8) * 8 + ((i // 2 + gap) % 4) * 2 + i % 2)


def along_z(block, gap):
    return move(block, lambda i: (i + 8 * gap) % 64)


def across(block):
    return move(block, lambda i: i ^ 1)


def digit_moves(message, stride):
    return [
        move(message, lambda i: i - ((i // stride) % 4) * stride + ((i // stride + k) % 4) * stride)
        for k in (3, 2, 1)
    ]


def around(block, gap):
    return lax.ppermute(block, "ch", [(i, (i + gap) % 4) for i in range(4)])


def after(parts, earlier):
    return lax.optimization_barrier((parts, earlier))[0]


def project(turns, mixed, gathered, other, earlier):
    return pl.pallas_call(
        lambda *refs: project_kernel(turns, *refs),
        out_shape=(b16(ROWS, QUARTER),) * (2 * len(turns)),
        in_specs=[WHOLE] * 3 + [FAR] * 2,
        out_specs=(WHOLE,) * (2 * len(turns)),
        scratch_shapes=[pltpu.VMEM((len(turns), HALF, WIDTH), jnp.bfloat16)],
        compiler_params=pltpu.CompilerParams(vmem_limit_bytes=LIMIT),
        cost_estimate=pl.CostEstimate(
            flops=len(turns) * 2 * ROWS * HALF * WIDTH,
            bytes_accessed=len(turns) * 4 * HALF * WIDTH, transcendentals=0),
    )(mixed, gathered, other, *earlier)


def reduced(mixed, gathered, other, orders):
    opposite_a, opposite_b = project((2,), mixed, gathered, other, orders[0])
    from_left, from_right = around(opposite_a, 1), around(opposite_b, -1)
    next_a, next_b, previous_a, previous_b = project(
        (1, 3), mixed, gathered, other, orders[1] or (opposite_a, opposite_b))
    one_b, one_a = around(next_b, 1), around(previous_a, -1)
    own_a, own_b = project((0,), mixed, gathered, other, orders[2] or (next_a, next_b))
    to_right, to_left = call(add_kernel, (b16(ROWS, QUARTER),) * 2, [WHOLE] * 4)(
        from_left, next_a, from_right, previous_b)
    sum_a, sum_b = around(to_right, 1), around(to_left, -1)
    return (own_a, own_b, sum_a, sum_b, one_a, one_b), to_right


def local(q_feat, k_feat, v_feat, short_taps, decay_rate, residue, skip_gain, out_weight,
          doc_starts, reset_flags):
    count = lax.axis_size("seq")
    tail_rows = pl.BlockSpec((16, WIDTH), lambda i: (ROWS // 16 - 1, 0))
    whole_shard = pl.BlockSpec((SHARD, WIDTH), lambda i: (0, 0))
    tails, shard = pl.pallas_call(
        tail_kernel,
        grid=(1,),
        out_shape=(f32(8, WIDTH), b16(SHARD, WIDTH)),
        in_specs=[SMALL] + [tail_rows] * 3 + [whole_shard],
        out_specs=(pl.BlockSpec((8, WIDTH), lambda i: (0, 0)), whole_shard),
    )(doc_starts, q_feat, k_feat, v_feat, out_weight)
    halo = lax.ppermute(tails, "seq", [(i, i + 1) for i in range(count - 1)])

    column = call(column_kernel, b16(2 * SHARD, WIDTH), [WHOLE] * 2 + [FAR])(
        shard, along_y(shard, 2), halo)
    right, left = [along_z(column, 1)], [along_z(column, 7)]

    def relay(earlier):
        ahead, behind = after((right[-1], left[-1]), earlier)
        right.append(along_z(ahead, 1))
        left.append(along_z(behind, 7))

    q_rows, gated, message = call(
        front_kernel,
        (f32(ROWS * GROUPS, LANES), f32(ROWS * GROUPS, LANES), f32(STATE + GROUPS, LANES)),
        [SMALL] * 2 + [FAR] * 3 + [WHOLE] * 3,
        scratch=[
            pltpu.VMEM((3, ROWS, WIDTH), jnp.bfloat16),
            pltpu.VMEM((3, ROWS + 8, WIDTH), jnp.float32),
            pltpu.VMEM((STATE, LANES), jnp.float32),
            pltpu.SemaphoreType.DMA((3,)),
        ],
        flops=20_000_000,
        moved=4_000_000,
    )(doc_starts, reset_flags, q_feat, k_feat, v_feat, halo, short_taps, decay_rate)

    pole_scratch = pltpu.VMEM((STATE, LANES), jnp.float32)
    two_messages = (f32(STATE + GROUPS, LANES), f32(STATE + GROUPS, LANES))
    low, following = call(low_kernel, two_messages, [WHOLE] * 5, scratch=[pole_scratch])(
        message, *digit_moves(message, 1), decay_rate)
    relay(message)
    relay(following)
    before, final = call(middle_kernel, two_messages, [WHOLE] * 6, scratch=[pole_scratch])(
        following, *digit_moves(following, 4), low, decay_rate)
    high = [
        lax.ppermute(final, "seq", [(i, i + k * 16) for i in range(count - k * 16)])
        for k in (3, 2, 1)
    ]
    ahead, behind = after((right[-1][:SHARD], left[-1][SHARD:]), final)
    parts = [column] + right + [along_z(ahead, 1), along_z(behind, 7)] + left[::-1]
    gathered = jnp.concatenate(after(parts, high), axis=0)
    other = across(gathered)
    mixed = call(
        mix_kernel,
        b16(ROWS, WIDTH),
        [SMALL] * 2 + [WHOLE] * 9,
        scratch=[pole_scratch, pole_scratch, pltpu.VMEM((ROWS * GROUPS, LANES), jnp.float32)],
        flops=20_000_000,
        moved=4_000_000,
    )(doc_starts, reset_flags, *high, before, decay_rate, residue, skip_gain[None, :], q_rows, gated)

    mate = move(mixed, lambda i: i ^ 2)
    mine, done = reduced(mixed, gathered, other, ((decay_rate, residue), None, None))
    parts, _ = reduced(mate, gathered, other, ((done, mine[0]), mine[4:], mine[2:4]))
    theirs = call(total_kernel, b16(ROWS, HALF), [WHOLE] * 6)(*parts)
    back = move(theirs, lambda i: i ^ 2)
    return call(last_kernel, b16(ROWS, WIDTH), [WHOLE] * 7)(*mine, back)


def solution(mesh):
    placed = (
        P("seq", "ch"),
        P("seq", "ch"),
        P("seq", "ch"),
        P(None, None, "ch"),
        P(None, "ch"),
        P(None, "ch"),
        P("ch"),
        P("seq", "ch"),
        P("seq", None),
        P("seq", None),
    )
    return jax.shard_map(
        local, mesh=mesh, in_specs=placed, out_specs=P("seq", "ch"), check_vma=False
    )
```

```python
import jax
import jax.numpy as jnp
from jax import lax
from jax.experimental import pallas as pl
from jax.experimental.pallas import tpu as pltpu
from jax.sharding import PartitionSpec as P

MODES = 16
ROWS = 256
LANES = 128
GROUPS = 8
WIDTH = GROUPS * LANES
STEPS = 8
CHUNKS = ROWS // STEPS
PIECE = 64
STATE = MODES * GROUPS
SHARD = 64
HALF = WIDTH // 2
QUARTER = WIDTH // 4


def reset_place(starts_ref, flags_ref):
    place = jnp.int32(0)
    found = jnp.int32(0)
    for slot in range(4):
        hit = (flags_ref[0, slot] == 1) & (starts_ref[0, slot] < ROWS)
        place = jnp.where(hit, starts_ref[0, slot], place)
        found = jnp.where(hit, jnp.int32(1), found)
    return place, found


def row_slice(t):
    return pl.ds(pl.multiple_of(t * GROUPS, GROUPS), GROUPS)


def spread(source, scratch):
    for group in range(GROUPS):
        scratch[pl.ds(group, MODES, stride=GROUPS), :] = source[:, group * LANES : (group + 1) * LANES]


def poles(ref):
    return [ref[n * GROUPS : (n + 1) * GROUPS, :] for n in range(MODES)]


def tail_kernel(starts_ref, q_ref, k_ref, v_ref, shard_ref, out_ref, shard_out):
    ends = starts_ref[0, 0] == ROWS - 1
    for slot in range(1, 4):
        ends = ends | (starts_ref[0, slot] == ROWS - 1)
    scale = jnp.where(ends, 0.0, 1.0)
    for which, source in enumerate((q_ref, k_ref, v_ref)):
        rows = source[...].astype(jnp.float32)
        out_ref[2 * which : 2 * which + 1, :] = rows[14:15, :] * scale
        out_ref[2 * which + 1 : 2 * which + 2, :] = rows[15:16, :]
    out_ref[6:8, :] = jnp.zeros((2, WIDTH), jnp.float32)
    shard_out[...] = shard_ref[...]


def column_kernel(shard_ref, far_ref, halo_ref, out_ref):
    del halo_ref
    out_ref[:SHARD, :] = shard_ref[...]
    out_ref[SHARD:, :] = far_ref[...]


def front_kernel(starts_ref, flags_ref, q_hbm, k_hbm, v_hbm, halo_ref, taps_ref, rate_ref,
                 q_out, gated_out, state_out, held, wide, spread_rate, sems):
    copies = [
        pltpu.make_async_copy(source, held.at[feature], sems.at[feature])
        for feature, source in enumerate((k_hbm, v_hbm, q_hbm))
    ]
    for copy in copies:
        copy.start()
    spread(rate_ref, spread_rate)
    for feature in range(3):
        which = (1, 2, 0)[feature]
        wide[feature, 6:8, :] = halo_ref[2 * which : 2 * which + 2, :]
        copies[feature].wait()
        wide[feature, 8:, :] = held[feature].astype(jnp.float32)
    for first in range(0, ROWS, PIECE):
        t = lax.broadcasted_iota(jnp.int32, (PIECE, LANES), 0) + first
        keep_one = jnp.ones((PIECE, LANES), jnp.float32)
        keep_two = keep_one
        for slot in range(4):
            at = starts_ref[0, slot]
            keep_one = jnp.where(t == at, 0.0, keep_one)
            keep_two = jnp.where((t == at) | (t == at + 1), 0.0, keep_two)
        for group in range(GROUPS):
            lanes = slice(group * LANES, (group + 1) * LANES)

            def short(feature, which):
                total = taps_ref[which, 0:1, lanes] * wide[feature, 8 + first : 8 + first + PIECE, lanes]
                total = total + (taps_ref[which, 1:2, lanes] * keep_one) * wide[
                    feature, 7 + first : 7 + first + PIECE, lanes]
                total = total + (taps_ref[which, 2:3, lanes] * keep_two) * wide[
                    feature, 6 + first : 6 + first + PIECE, lanes]
                return total.astype(jnp.bfloat16).astype(jnp.float32)

            rows = pl.ds(first * GROUPS + group, PIECE, stride=GROUPS)
            gated_out[rows, :] = short(0, 1) * short(1, 2)
            q_out[rows, :] = short(2, 0)
    place, found = reset_place(starts_ref, flags_ref)
    decay = [jnp.exp(-rate) for rate in poles(spread_rate)]

    def chunk(index, state):
        for step in range(STEPS):
            t = index * STEPS + step
            row = jnp.where(t >= place, gated_out[row_slice(t), :], 0.0)
            state = tuple(decay[n] * state[n] + row for n in range(MODES))
        return state

    zero = jnp.zeros((GROUPS, LANES), jnp.float32)
    state = lax.fori_loop(place // STEPS, CHUNKS, chunk, (zero,) * MODES)
    for n in range(MODES):
        state_out[n * GROUPS : (n + 1) * GROUPS, :] = state[n]
    state_out[STATE:, :] = jnp.full((GROUPS, LANES), 1 - found, jnp.int32).astype(jnp.float32)


def digit_join(mine, got, length, spread_rate, total=None, own=None):
    entering, whole = [], []
    alive = jnp.ones((GROUPS, LANES), jnp.float32)
    whole_alive = alive
    flags = [ref[STATE:, :] for ref in got]
    for k, flag in zip((3, 2, 1), flags):
        alive = alive * jnp.where(k <= mine, flag, 1.0)
    for n in range(MODES):
        rows = slice(n * GROUPS, (n + 1) * GROUPS)
        passing = jnp.exp(-length * spread_rate[rows, :])
        value = jnp.zeros((GROUPS, LANES), jnp.float32)
        for k, ref, flag in zip((3, 2, 1), got, flags):
            value = jnp.where(k <= mine, ref[rows, :] + passing * flag * value, 0.0)
        entering.append(value)
        if own is not None:
            value = own[rows, :] + passing * own[STATE:, :] * value
            for k, ref, flag in zip((3, 2, 1), got, flags):
                value = jnp.where(k > mine, ref[rows, :] + passing * flag * value, value)
            whole.append(value)
    if own is not None:
        whole_alive = own[STATE:, :] * flags[0] * flags[1] * flags[2]
    return entering, alive, whole, whole_alive


def low_kernel(own, got3, got2, got1, rate_ref, enter_out, next_out, spread_rate):
    spread(rate_ref, spread_rate)
    mine = lax.axis_index("seq") % 4
    entering, alive, whole, whole_alive = digit_join(
        mine, (got3, got2, got1), 256.0, spread_rate, own=own)
    for n in range(MODES):
        enter_out[n * GROUPS : (n + 1) * GROUPS, :] = entering[n]
        next_out[n * GROUPS : (n + 1) * GROUPS, :] = whole[n]
    enter_out[STATE:, :] = alive
    next_out[STATE:, :] = whole_alive


def middle_kernel(own, got3, got2, got1, low, rate_ref, enter_out, next_out, spread_rate):
    spread(rate_ref, spread_rate)
    seq = lax.axis_index("seq")
    entering, alive, whole, whole_alive = digit_join(
        (seq // 4) % 4, (got3, got2, got1), 1024.0, spread_rate, own=own)
    span = (seq % 4).astype(jnp.float32) * 256.0
    low_alive = low[STATE:, :]
    for n in range(MODES):
        rows = slice(n * GROUPS, (n + 1) * GROUPS)
        reach = jnp.exp(-span * spread_rate[rows, :]) * low_alive
        enter_out[rows, :] = low[rows, :] + reach * entering[n]
        next_out[rows, :] = whole[n]
    enter_out[STATE:, :] = alive * low_alive
    next_out[STATE:, :] = whole_alive


def mix_kernel(starts_ref, flags_ref, got3, got2, got1, before, rate_ref, residue_ref, skip_ref,
               q_ref, gated_ref, mixed_out, spread_rate, spread_gain, rows_ref):
    spread(rate_ref, spread_rate)
    spread(residue_ref, spread_gain)
    skip = jnp.concatenate(
        [skip_ref[:, group * LANES : (group + 1) * LANES] for group in range(GROUPS)], axis=0)
    seq = lax.axis_index("seq")
    entering, _, _, _ = digit_join(seq // 16, (got3, got2, got1), 4096.0, spread_rate)
    span = (seq % 16).astype(jnp.float32) * 256.0
    before_alive = before[STATE:, :]
    state, decay = [], []
    for n, rate in enumerate(poles(spread_rate)):
        rows = slice(n * GROUPS, (n + 1) * GROUPS)
        state.append(before[rows, :] + jnp.exp(-span * rate) * before_alive * entering[n])
        decay.append(jnp.exp(-rate))
    state = tuple(state)
    weight = poles(spread_gain)
    place, found = reset_place(starts_ref, flags_ref)
    cut_chunk = jnp.where(found == 1, place // STEPS, CHUNKS)

    def run(index, state, cutting):
        for step in range(STEPS):
            t = index * STEPS + step
            row = gated_ref[row_slice(t), :]
            if cutting:
                state = tuple(jnp.where(t == place, 0.0, state[n]) for n in range(MODES))
            state = tuple(decay[n] * state[n] + row for n in range(MODES))
            terms = [weight[n] * state[n] for n in range(MODES)] + [skip * row]
            while len(terms) > 1:
                paired = [terms[i] + terms[i + 1] for i in range(0, len(terms) - 1, 2)]
                terms = paired + terms[len(terms) - len(terms) % 2 :]
            rows_ref[row_slice(t), :] = q_ref[row_slice(t), :] * terms[0]
        return state

    state = lax.fori_loop(0, cut_chunk, lambda i, s: run(i, s, False), state)
    state = lax.fori_loop(
        cut_chunk, jnp.minimum(cut_chunk + 1, CHUNKS), lambda i, s: run(i, s, True), state)
    lax.fori_loop(cut_chunk + 1, CHUNKS, lambda i, s: run(i, s, False), state)
    for group in range(GROUPS):
        mixed_out[:, group * LANES : (group + 1) * LANES] = rows_ref[
            pl.ds(group, ROWS, stride=GROUPS), :].astype(jnp.bfloat16)


def project_kernel(turns, mixed_ref, gathered, other, earlier, before, *refs):
    del earlier, before
    outs, weight = refs[: 2 * len(turns)], refs[2 * len(turns)]
    seq, ch = lax.axis_index("seq"), lax.axis_index("ch")
    z, y, core = seq // 8, (seq // 2) % 4, seq % 2
    for slot, turn in enumerate(turns):
        target = (ch + turn) % 4
        for side, source in enumerate((gathered, other)):
            at_core = (core + side) % 2
            for half in range(2):
                age = (z - 2 * target - half + 16) % 8
                for gap in range(2):
                    at_y = (y // 2 + gap) % 2
                    row = pl.multiple_of(((half * 2 + at_y) * 2 + at_core) * SHARD, SHARD)
                    start = pl.multiple_of((age * 2 + gap) * SHARD, SHARD)
                    weight[slot, pl.ds(row, SHARD), :] = source[pl.ds(start, SHARD), :]
        for part in range(2):
            outs[2 * slot + part][...] = lax.dot_general(
                mixed_ref[...], weight[slot, part * QUARTER : (part + 1) * QUARTER, :],
                (((1,), (1,)), ((), ())), preferred_element_type=jnp.float32).astype(jnp.bfloat16)


def add_kernel(right_ref, right_own, left_ref, left_own, right_out, left_out):
    right_out[...] = (right_ref[...].astype(jnp.float32) + right_own[...].astype(jnp.float32)).astype(jnp.bfloat16)
    left_out[...] = (left_ref[...].astype(jnp.float32) + left_own[...].astype(jnp.float32)).astype(jnp.bfloat16)


def summed(own_a, own_b, sum_a, sum_b, one_a, one_b, part):
    chosen = ((own_a, sum_a, one_a), (own_b, sum_b, one_b))[part]
    first, second, third = [ref[...].astype(jnp.float32) for ref in chosen]
    return (first + second + third).astype(jnp.bfloat16)


def total_kernel(*refs):
    for part in range(2):
        refs[6][:, part * QUARTER : (part + 1) * QUARTER] = summed(*refs[:6], part)


def last_kernel(*refs):
    mate, out_ref = refs[6], refs[7]
    parity = (lax.axis_index("seq") // 2) % 2
    for part in range(2):
        mine = summed(*refs[:6], part)
        for at_y in range(2):
            block = 4 * part + 2 * at_y
            lanes = slice(at_y * LANES, (at_y + 1) * LANES)
            out_ref[:, pl.ds(pl.multiple_of((block + parity) * LANES, LANES), LANES)] = mine[:, lanes]
            lanes = slice((2 * part + at_y) * LANES, (2 * part + at_y + 1) * LANES)
            out_ref[:, pl.ds(pl.multiple_of((block + 1 - parity) * LANES, LANES), LANES)] = mate[:, lanes]


SMALL = pl.BlockSpec(memory_space=pltpu.SMEM)
WHOLE = pl.BlockSpec(memory_space=pltpu.VMEM)
FAR = pl.BlockSpec(memory_space=pl.ANY)
LIMIT = 40 * 1024 * 1024


def call(kernel, outs, specs, scratch=(), flops=4_000_000, moved=2_000_000):
    return pl.pallas_call(
        kernel,
        out_shape=outs,
        in_specs=specs,
        out_specs=jax.tree.map(lambda _: WHOLE, outs),
        scratch_shapes=scratch,
        compiler_params=pltpu.CompilerParams(vmem_limit_bytes=LIMIT),
        cost_estimate=pl.CostEstimate(flops=flops, bytes_accessed=moved, transcendentals=0),
    )


def f32(*shape):
    return jax.ShapeDtypeStruct(shape, jnp.float32)


def b16(*shape):
    return jax.ShapeDtypeStruct(shape, jnp.bfloat16)


def move(block, target):
    count = lax.axis_size("seq")
    return lax.ppermute(block, "seq", [(i, target(i)) for i in range(count)])


def along_y(block, gap):
    return move(block, lambda i: (i // 8) * 8 + ((i // 2 + gap) % 4) * 2 + i % 2)


def along_z(block, gap):
    return move(block, lambda i: (i + 8 * gap) % 64)


def across(block):
    return move(block, lambda i: i ^ 1)


def digit_moves(message, stride):
    return [
        move(message, lambda i: i - ((i // stride) % 4) * stride + ((i // stride + k) % 4) * stride)
        for k in (3, 2, 1)
    ]


def around(block, gap):
    return lax.ppermute(block, "ch", [(i, (i + gap) % 4) for i in range(4)])


def after(parts, earlier):
    return lax.optimization_barrier((parts, earlier))[0]


def project(turns, mixed, gathered, other, earlier):
    return pl.pallas_call(
        lambda *refs: project_kernel(turns, *refs),
        out_shape=(b16(ROWS, QUARTER),) * (2 * len(turns)),
        in_specs=[WHOLE] * 3 + [FAR] * 2,
        out_specs=(WHOLE,) * (2 * len(turns)),
        scratch_shapes=[pltpu.VMEM((len(turns), HALF, WIDTH), jnp.bfloat16)],
        compiler_params=pltpu.CompilerParams(vmem_limit_bytes=LIMIT),
        cost_estimate=pl.CostEstimate(
            flops=len(turns) * 2 * ROWS * HALF * WIDTH,
            bytes_accessed=len(turns) * 4 * HALF * WIDTH, transcendentals=0),
    )(mixed, gathered, other, *earlier)


def reduced(mixed, gathered, other, orders):
    opposite_a, opposite_b = project((2,), mixed, gathered, other, orders[0])
    from_left, from_right = around(opposite_a, 1), around(opposite_b, -1)
    next_a, next_b, previous_a, previous_b = project(
        (1, 3), mixed, gathered, other, orders[1] or (opposite_a, opposite_b))
    one_b, one_a = around(next_b, 1), around(previous_a, -1)
    own_a, own_b = project((0,), mixed, gathered, other, orders[2] or (next_a, next_b))
    to_right, to_left = call(add_kernel, (b16(ROWS, QUARTER),) * 2, [WHOLE] * 4)(
        from_left, next_a, from_right, previous_b)
    sum_a, sum_b = around(to_right, 1), around(to_left, -1)
    return (own_a, own_b, sum_a, sum_b, one_a, one_b), to_right


def local(q_feat, k_feat, v_feat, short_taps, decay_rate, residue, skip_gain, out_weight,
          doc_starts, reset_flags):
    count = lax.axis_size("seq")
    tail_rows = pl.BlockSpec((16, WIDTH), lambda i: (ROWS // 16 - 1, 0))
    whole_shard = pl.BlockSpec((SHARD, WIDTH), lambda i: (0, 0))
    tails, shard = pl.pallas_call(
        tail_kernel,
        grid=(1,),
        out_shape=(f32(8, WIDTH), b16(SHARD, WIDTH)),
        in_specs=[SMALL] + [tail_rows] * 3 + [whole_shard],
        out_specs=(pl.BlockSpec((8, WIDTH), lambda i: (0, 0)), whole_shard),
    )(doc_starts, q_feat, k_feat, v_feat, out_weight)
    halo = lax.ppermute(tails, "seq", [(i, i + 1) for i in range(count - 1)])

    column = call(column_kernel, b16(2 * SHARD, WIDTH), [WHOLE] * 2 + [FAR])(
        shard, along_y(shard, 2), halo)
    right, left = [along_z(column, 1)], [along_z(column, 7)]

    def relay(earlier):
        ahead, behind = after((right[-1], left[-1]), earlier)
        right.append(along_z(ahead, 1))
        left.append(along_z(behind, 7))

    q_rows, gated, message = call(
        front_kernel,
        (f32(ROWS * GROUPS, LANES), f32(ROWS * GROUPS, LANES), f32(STATE + GROUPS, LANES)),
        [SMALL] * 2 + [FAR] * 3 + [WHOLE] * 3,
        scratch=[
            pltpu.VMEM((3, ROWS, WIDTH), jnp.bfloat16),
            pltpu.VMEM((3, ROWS + 8, WIDTH), jnp.float32),
            pltpu.VMEM((STATE, LANES), jnp.float32),
            pltpu.SemaphoreType.DMA((3,)),
        ],
        flops=20_000_000,
        moved=4_000_000,
    )(doc_starts, reset_flags, q_feat, k_feat, v_feat, halo, short_taps, decay_rate)

    pole_scratch = pltpu.VMEM((STATE, LANES), jnp.float32)
    two_messages = (f32(STATE + GROUPS, LANES), f32(STATE + GROUPS, LANES))
    low, following = call(low_kernel, two_messages, [WHOLE] * 5, scratch=[pole_scratch])(
        message, *digit_moves(message, 1), decay_rate)
    middle_moves = digit_moves(following, 4)
    relay(following)
    opposite = [along_z(after(right[1][:SHARD], following), 2), along_z(after(left[1][SHARD:], following), 6)]
    relay(following)
    before, final = call(middle_kernel, two_messages, [WHOLE] * 6, scratch=[pole_scratch])(
        following, *middle_moves, low, decay_rate)
    high = [
        lax.ppermute(final, "seq", [(i, i + k * 16) for i in range(count - k * 16)])
        for k in (3, 2, 1)
    ]
    parts = [column] + right + opposite + left[::-1]
    gathered = jnp.concatenate(after(parts, high), axis=0)
    other = across(gathered)
    mixed = call(
        mix_kernel,
        b16(ROWS, WIDTH),
        [SMALL] * 2 + [WHOLE] * 9,
        scratch=[pole_scratch, pole_scratch, pltpu.VMEM((ROWS * GROUPS, LANES), jnp.float32)],
        flops=20_000_000,
        moved=4_000_000,
    )(doc_starts, reset_flags, *high, before, decay_rate, residue, skip_gain[None, :], q_rows, gated)

    mate = move(mixed, lambda i: i ^ 2)
    mine, done = reduced(mixed, gathered, other, ((decay_rate, residue), None, None))
    parts, _ = reduced(mate, gathered, other, ((done, mine[0]), mine[4:], mine[2:4]))
    theirs = call(total_kernel, b16(ROWS, HALF), [WHOLE] * 6)(*parts)
    back = move(theirs, lambda i: i ^ 2)
    return call(last_kernel, b16(ROWS, WIDTH), [WHOLE] * 7)(*mine, back)


def solution(mesh):
    placed = (
        P("seq", "ch"),
        P("seq", "ch"),
        P("seq", "ch"),
        P(None, None, "ch"),
        P(None, "ch"),
        P(None, "ch"),
        P("ch"),
        P("seq", "ch"),
        P("seq", None),
        P("seq", None),
    )
    return jax.shard_map(
        local, mesh=mesh, in_specs=placed, out_specs=P("seq", "ch"), check_vma=False
    )
```

```python
import jax
import jax.numpy as jnp
from jax import lax
from jax.experimental import pallas as pl
from jax.experimental.pallas import tpu as pltpu
from jax.sharding import PartitionSpec as P

MODES = 16
ROWS = 256
LANES = 128
GROUPS = 8
WIDTH = GROUPS * LANES
STEPS = 16
CHUNKS = ROWS // STEPS
PIECE = 64
STATE = MODES * GROUPS
SHARD = 64
HALF = WIDTH // 2
QUARTER = WIDTH // 4


def reset_place(starts_ref, flags_ref):
    place = jnp.int32(0)
    found = jnp.int32(0)
    for slot in range(4):
        hit = (flags_ref[0, slot] == 1) & (starts_ref[0, slot] < ROWS)
        place = jnp.where(hit, starts_ref[0, slot], place)
        found = jnp.where(hit, jnp.int32(1), found)
    return place, found


def row_slice(t):
    return pl.ds(pl.multiple_of(t * GROUPS, GROUPS), GROUPS)


def spread(source, scratch):
    for group in range(GROUPS):
        scratch[pl.ds(group, MODES, stride=GROUPS), :] = source[:, group * LANES : (group + 1) * LANES]


def poles(ref):
    return [ref[n * GROUPS : (n + 1) * GROUPS, :] for n in range(MODES)]


def tail_kernel(starts_ref, q_ref, k_ref, v_ref, shard_ref, out_ref, shard_out):
    ends = starts_ref[0, 0] == ROWS - 1
    for slot in range(1, 4):
        ends = ends | (starts_ref[0, slot] == ROWS - 1)
    scale = jnp.where(ends, 0.0, 1.0)
    for which, source in enumerate((q_ref, k_ref, v_ref)):
        rows = source[...].astype(jnp.float32)
        out_ref[2 * which : 2 * which + 1, :] = rows[14:15, :] * scale
        out_ref[2 * which + 1 : 2 * which + 2, :] = rows[15:16, :]
    out_ref[6:8, :] = jnp.zeros((2, WIDTH), jnp.float32)
    shard_out[...] = shard_ref[...]


def column_kernel(shard_ref, far_ref, halo_ref, out_ref):
    del halo_ref
    out_ref[:SHARD, :] = shard_ref[...]
    out_ref[SHARD:, :] = far_ref[...]


def front_kernel(starts_ref, flags_ref, q_hbm, k_hbm, v_hbm, halo_ref, taps_ref, rate_ref,
                 q_out, gated_out, state_out, held, wide, spread_rate, sems):
    copies = [
        pltpu.make_async_copy(source, held.at[feature], sems.at[feature])
        for feature, source in enumerate((k_hbm, v_hbm, q_hbm))
    ]
    for copy in copies:
        copy.start()
    spread(rate_ref, spread_rate)
    for feature in range(3):
        which = (1, 2, 0)[feature]
        wide[feature, 6:8, :] = halo_ref[2 * which : 2 * which + 2, :]
        copies[feature].wait()
        wide[feature, 8:, :] = held[feature].astype(jnp.float32)
    for first in range(0, ROWS, PIECE):
        t = lax.broadcasted_iota(jnp.int32, (PIECE, LANES), 0) + first
        keep_one = jnp.ones((PIECE, LANES), jnp.float32)
        keep_two = keep_one
        for slot in range(4):
            at = starts_ref[0, slot]
            keep_one = jnp.where(t == at, 0.0, keep_one)
            keep_two = jnp.where((t == at) | (t == at + 1), 0.0, keep_two)
        for group in range(GROUPS):
            lanes = slice(group * LANES, (group + 1) * LANES)

            def short(feature, which):
                total = taps_ref[which, 0:1, lanes] * wide[feature, 8 + first : 8 + first + PIECE, lanes]
                total = total + (taps_ref[which, 1:2, lanes] * keep_one) * wide[
                    feature, 7 + first : 7 + first + PIECE, lanes]
                total = total + (taps_ref[which, 2:3, lanes] * keep_two) * wide[
                    feature, 6 + first : 6 + first + PIECE, lanes]
                return total.astype(jnp.bfloat16).astype(jnp.float32)

            rows = pl.ds(first * GROUPS + group, PIECE, stride=GROUPS)
            gated_out[rows, :] = short(0, 1) * short(1, 2)
            q_out[rows, :] = short(2, 0)
    place, found = reset_place(starts_ref, flags_ref)
    decay = [jnp.exp(-rate) for rate in poles(spread_rate)]

    def chunk(index, state):
        for step in range(STEPS):
            t = index * STEPS + step
            row = jnp.where(t >= place, gated_out[row_slice(t), :], 0.0)
            state = tuple(decay[n] * state[n] + row for n in range(MODES))
        return state

    zero = jnp.zeros((GROUPS, LANES), jnp.float32)
    state = lax.fori_loop(place // STEPS, CHUNKS, chunk, (zero,) * MODES)
    for n in range(MODES):
        state_out[n * GROUPS : (n + 1) * GROUPS, :] = state[n]
    state_out[STATE:, :] = jnp.full((GROUPS, LANES), 1 - found, jnp.int32).astype(jnp.float32)


def digit_join(mine, got, length, spread_rate, total=None, own=None):
    entering, whole = [], []
    alive = jnp.ones((GROUPS, LANES), jnp.float32)
    whole_alive = alive
    flags = [ref[STATE:, :] for ref in got]
    for k, flag in zip((3, 2, 1), flags):
        alive = alive * jnp.where(k <= mine, flag, 1.0)
    for n in range(MODES):
        rows = slice(n * GROUPS, (n + 1) * GROUPS)
        passing = jnp.exp(-length * spread_rate[rows, :])
        value = jnp.zeros((GROUPS, LANES), jnp.float32)
        for k, ref, flag in zip((3, 2, 1), got, flags):
            value = jnp.where(k <= mine, ref[rows, :] + passing * flag * value, 0.0)
        entering.append(value)
        if own is not None:
            value = own[rows, :] + passing * own[STATE:, :] * value
            for k, ref, flag in zip((3, 2, 1), got, flags):
                value = jnp.where(k > mine, ref[rows, :] + passing * flag * value, value)
            whole.append(value)
    if own is not None:
        whole_alive = own[STATE:, :] * flags[0] * flags[1] * flags[2]
    return entering, alive, whole, whole_alive


def low_kernel(own, got3, got2, got1, rate_ref, enter_out, next_out, spread_rate):
    spread(rate_ref, spread_rate)
    mine = lax.axis_index("seq") % 4
    entering, alive, whole, whole_alive = digit_join(
        mine, (got3, got2, got1), 256.0, spread_rate, own=own)
    for n in range(MODES):
        enter_out[n * GROUPS : (n + 1) * GROUPS, :] = entering[n]
        next_out[n * GROUPS : (n + 1) * GROUPS, :] = whole[n]
    enter_out[STATE:, :] = alive
    next_out[STATE:, :] = whole_alive


def middle_kernel(own, got3, got2, got1, low, rate_ref, enter_out, next_out, spread_rate):
    spread(rate_ref, spread_rate)
    seq = lax.axis_index("seq")
    entering, alive, whole, whole_alive = digit_join(
        (seq // 4) % 4, (got3, got2, got1), 1024.0, spread_rate, own=own)
    span = (seq % 4).astype(jnp.float32) * 256.0
    low_alive = low[STATE:, :]
    for n in range(MODES):
        rows = slice(n * GROUPS, (n + 1) * GROUPS)
        reach = jnp.exp(-span * spread_rate[rows, :]) * low_alive
        enter_out[rows, :] = low[rows, :] + reach * entering[n]
        next_out[rows, :] = whole[n]
    enter_out[STATE:, :] = alive * low_alive
    next_out[STATE:, :] = whole_alive


def mix_kernel(starts_ref, flags_ref, got3, got2, got1, before, rate_ref, residue_ref, skip_ref,
               q_ref, gated_ref, mixed_out, spread_rate, spread_gain, rows_ref):
    spread(rate_ref, spread_rate)
    spread(residue_ref, spread_gain)
    skip = jnp.concatenate(
        [skip_ref[:, group * LANES : (group + 1) * LANES] for group in range(GROUPS)], axis=0)
    seq = lax.axis_index("seq")
    entering, _, _, _ = digit_join(seq // 16, (got3, got2, got1), 4096.0, spread_rate)
    span = (seq % 16).astype(jnp.float32) * 256.0
    before_alive = before[STATE:, :]
    state, decay = [], []
    for n, rate in enumerate(poles(spread_rate)):
        rows = slice(n * GROUPS, (n + 1) * GROUPS)
        state.append(before[rows, :] + jnp.exp(-span * rate) * before_alive * entering[n])
        decay.append(jnp.exp(-rate))
    state = tuple(state)
    weight = poles(spread_gain)
    place, found = reset_place(starts_ref, flags_ref)
    cut_chunk = jnp.where(found == 1, place // STEPS, CHUNKS)

    def run(index, state, cutting):
        for step in range(STEPS):
            t = index * STEPS + step
            row = gated_ref[row_slice(t), :]
            if cutting:
                state = tuple(jnp.where(t == place, 0.0, state[n]) for n in range(MODES))
            state = tuple(decay[n] * state[n] + row for n in range(MODES))
            terms = [weight[n] * state[n] for n in range(MODES)] + [skip * row]
            while len(terms) > 1:
                paired = [terms[i] + terms[i + 1] for i in range(0, len(terms) - 1, 2)]
                terms = paired + terms[len(terms) - len(terms) % 2 :]
            rows_ref[row_slice(t), :] = q_ref[row_slice(t), :] * terms[0]
        return state

    state = lax.fori_loop(0, cut_chunk, lambda i, s: run(i, s, False), state)
    state = lax.fori_loop(
        cut_chunk, jnp.minimum(cut_chunk + 1, CHUNKS), lambda i, s: run(i, s, True), state)
    lax.fori_loop(cut_chunk + 1, CHUNKS, lambda i, s: run(i, s, False), state)
    for group in range(GROUPS):
        mixed_out[:, group * LANES : (group + 1) * LANES] = rows_ref[
            pl.ds(group, ROWS, stride=GROUPS), :].astype(jnp.bfloat16)


def project_kernel(turns, mixed_ref, gathered, other, earlier, before, *refs):
    del earlier, before
    outs, weight = refs[: 2 * len(turns)], refs[2 * len(turns)]
    seq, ch = lax.axis_index("seq"), lax.axis_index("ch")
    z, y, core = seq // 8, (seq // 2) % 4, seq % 2
    for slot, turn in enumerate(turns):
        target = (ch + turn) % 4
        for side, source in enumerate((gathered, other)):
            at_core = (core + side) % 2
            for half in range(2):
                age = (z - 2 * target - half + 16) % 8
                for gap in range(2):
                    at_y = (y // 2 + gap) % 2
                    row = pl.multiple_of(((half * 2 + at_y) * 2 + at_core) * SHARD, SHARD)
                    start = pl.multiple_of((age * 2 + gap) * SHARD, SHARD)
                    weight[slot, pl.ds(row, SHARD), :] = source[pl.ds(start, SHARD), :]
        for part in range(2):
            outs[2 * slot + part][...] = lax.dot_general(
                mixed_ref[...], weight[slot, part * QUARTER : (part + 1) * QUARTER, :],
                (((1,), (1,)), ((), ())), preferred_element_type=jnp.float32).astype(jnp.bfloat16)


def add_kernel(right_ref, right_own, left_ref, left_own, right_out, left_out):
    right_out[...] = (right_ref[...].astype(jnp.float32) + right_own[...].astype(jnp.float32)).astype(jnp.bfloat16)
    left_out[...] = (left_ref[...].astype(jnp.float32) + left_own[...].astype(jnp.float32)).astype(jnp.bfloat16)


def summed(own_a, own_b, sum_a, sum_b, one_a, one_b, part):
    chosen = ((own_a, sum_a, one_a), (own_b, sum_b, one_b))[part]
    first, second, third = [ref[...].astype(jnp.float32) for ref in chosen]
    return (first + second + third).astype(jnp.bfloat16)


def total_kernel(*refs):
    for part in range(2):
        refs[6][:, part * QUARTER : (part + 1) * QUARTER] = summed(*refs[:6], part)


def last_kernel(*refs):
    mate, out_ref = refs[6], refs[7]
    parity = (lax.axis_index("seq") // 2) % 2
    for part in range(2):
        mine = summed(*refs[:6], part)
        for at_y in range(2):
            block = 4 * part + 2 * at_y
            lanes = slice(at_y * LANES, (at_y + 1) * LANES)
            out_ref[:, pl.ds(pl.multiple_of((block + parity) * LANES, LANES), LANES)] = mine[:, lanes]
            lanes = slice((2 * part + at_y) * LANES, (2 * part + at_y + 1) * LANES)
            out_ref[:, pl.ds(pl.multiple_of((block + 1 - parity) * LANES, LANES), LANES)] = mate[:, lanes]


SMALL = pl.BlockSpec(memory_space=pltpu.SMEM)
WHOLE = pl.BlockSpec(memory_space=pltpu.VMEM)
FAR = pl.BlockSpec(memory_space=pl.ANY)
LIMIT = 40 * 1024 * 1024


def call(kernel, outs, specs, scratch=(), flops=4_000_000, moved=2_000_000):
    return pl.pallas_call(
        kernel,
        out_shape=outs,
        in_specs=specs,
        out_specs=jax.tree.map(lambda _: WHOLE, outs),
        scratch_shapes=scratch,
        compiler_params=pltpu.CompilerParams(vmem_limit_bytes=LIMIT),
        cost_estimate=pl.CostEstimate(flops=flops, bytes_accessed=moved, transcendentals=0),
    )


def f32(*shape):
    return jax.ShapeDtypeStruct(shape, jnp.float32)


def b16(*shape):
    return jax.ShapeDtypeStruct(shape, jnp.bfloat16)


def move(block, target):
    count = lax.axis_size("seq")
    return lax.ppermute(block, "seq", [(i, target(i)) for i in range(count)])


def along_y(block, gap):
    return move(block, lambda i: (i // 8) * 8 + ((i // 2 + gap) % 4) * 2 + i % 2)


def along_z(block, gap):
    return move(block, lambda i: (i + 8 * gap) % 64)


def across(block):
    return move(block, lambda i: i ^ 1)


def digit_moves(message, stride):
    return [
        move(message, lambda i: i - ((i // stride) % 4) * stride + ((i // stride + k) % 4) * stride)
        for k in (3, 2, 1)
    ]


def around(block, gap):
    return lax.ppermute(block, "ch", [(i, (i + gap) % 4) for i in range(4)])


def after(parts, earlier):
    return lax.optimization_barrier((parts, earlier))[0]


def project(turns, mixed, gathered, other, earlier):
    return pl.pallas_call(
        lambda *refs: project_kernel(turns, *refs),
        out_shape=(b16(ROWS, QUARTER),) * (2 * len(turns)),
        in_specs=[WHOLE] * 3 + [FAR] * 2,
        out_specs=(WHOLE,) * (2 * len(turns)),
        scratch_shapes=[pltpu.VMEM((len(turns), HALF, WIDTH), jnp.bfloat16)],
        compiler_params=pltpu.CompilerParams(vmem_limit_bytes=LIMIT),
        cost_estimate=pl.CostEstimate(
            flops=len(turns) * 2 * ROWS * HALF * WIDTH,
            bytes_accessed=len(turns) * 4 * HALF * WIDTH, transcendentals=0),
    )(mixed, gathered, other, *earlier)


def reduced(mixed, gathered, other, orders):
    opposite_a, opposite_b = project((2,), mixed, gathered, other, orders[0])
    from_left, from_right = around(opposite_a, 1), around(opposite_b, -1)
    next_a, next_b, previous_a, previous_b, own_a, own_b = project(
        (1, 3, 0), mixed, gathered, other, orders[1] or (opposite_a, opposite_b))
    one_b, one_a = around(next_b, 1), around(previous_a, -1)
    to_right, to_left = call(add_kernel, (b16(ROWS, QUARTER),) * 2, [WHOLE] * 4)(
        from_left, next_a, from_right, previous_b)
    sum_a, sum_b = around(to_right, 1), around(to_left, -1)
    return (own_a, own_b, sum_a, sum_b, one_a, one_b), to_right


def local(q_feat, k_feat, v_feat, short_taps, decay_rate, residue, skip_gain, out_weight,
          doc_starts, reset_flags):
    count = lax.axis_size("seq")
    tail_rows = pl.BlockSpec((16, WIDTH), lambda i: (ROWS // 16 - 1, 0))
    whole_shard = pl.BlockSpec((SHARD, WIDTH), lambda i: (0, 0))
    tails, shard = pl.pallas_call(
        tail_kernel,
        grid=(1,),
        out_shape=(f32(8, WIDTH), b16(SHARD, WIDTH)),
        in_specs=[SMALL] + [tail_rows] * 3 + [whole_shard],
        out_specs=(pl.BlockSpec((8, WIDTH), lambda i: (0, 0)), whole_shard),
    )(doc_starts, q_feat, k_feat, v_feat, out_weight)
    halo = lax.ppermute(tails, "seq", [(i, i + 1) for i in range(count - 1)])

    column = call(column_kernel, b16(2 * SHARD, WIDTH), [WHOLE] * 2 + [FAR])(
        shard, along_y(shard, 2), halo)
    right, left = [along_z(column, 1)], [along_z(column, 7)]

    def relay(earlier):
        ahead, behind = after((right[-1], left[-1]), earlier)
        right.append(along_z(ahead, 1))
        left.append(along_z(behind, 7))

    q_rows, gated, message = call(
        front_kernel,
        (f32(ROWS * GROUPS, LANES), f32(ROWS * GROUPS, LANES), f32(STATE + GROUPS, LANES)),
        [SMALL] * 2 + [FAR] * 3 + [WHOLE] * 3,
        scratch=[
            pltpu.VMEM((3, ROWS, WIDTH), jnp.bfloat16),
            pltpu.VMEM((3, ROWS + 8, WIDTH), jnp.float32),
            pltpu.VMEM((STATE, LANES), jnp.float32),
            pltpu.SemaphoreType.DMA((3,)),
        ],
        flops=20_000_000,
        moved=4_000_000,
    )(doc_starts, reset_flags, q_feat, k_feat, v_feat, halo, short_taps, decay_rate)

    pole_scratch = pltpu.VMEM((STATE, LANES), jnp.float32)
    two_messages = (f32(STATE + GROUPS, LANES), f32(STATE + GROUPS, LANES))
    low, following = call(low_kernel, two_messages, [WHOLE] * 5, scratch=[pole_scratch])(
        message, *digit_moves(message, 1), decay_rate)
    middle_moves = digit_moves(following, 4)
    relay(following)
    opposite = [along_z(after(right[1][:SHARD], following), 2), along_z(after(left[1][SHARD:], following), 6)]
    relay(following)
    before, final = call(middle_kernel, two_messages, [WHOLE] * 6, scratch=[pole_scratch])(
        following, *middle_moves, low, decay_rate)
    high = [
        lax.ppermute(final, "seq", [(i, i + k * 16) for i in range(count - k * 16)])
        for k in (3, 2, 1)
    ]
    parts = [column] + right + opposite + left[::-1]
    gathered = jnp.concatenate(after(parts, high), axis=0)
    other = across(gathered)
    mixed = call(
        mix_kernel,
        b16(ROWS, WIDTH),
        [SMALL] * 2 + [WHOLE] * 9,
        scratch=[pole_scratch, pole_scratch, pltpu.VMEM((ROWS * GROUPS, LANES), jnp.float32)],
        flops=20_000_000,
        moved=4_000_000,
    )(doc_starts, reset_flags, *high, before, decay_rate, residue, skip_gain[None, :], q_rows, gated)

    mate = move(mixed, lambda i: i ^ 2)
    mine, done = reduced(mixed, gathered, other, ((decay_rate, residue), None, None))
    parts, _ = reduced(mate, gathered, other, ((done, mine[0]), mine[4:], mine[2:4]))
    theirs = call(total_kernel, b16(ROWS, HALF), [WHOLE] * 6)(*parts)
    back = move(theirs, lambda i: i ^ 2)
    return call(last_kernel, b16(ROWS, WIDTH), [WHOLE] * 7)(*mine, back)


def solution(mesh):
    placed = (
        P("seq", "ch"),
        P("seq", "ch"),
        P("seq", "ch"),
        P(None, None, "ch"),
        P(None, "ch"),
        P(None, "ch"),
        P("ch"),
        P("seq", "ch"),
        P("seq", None),
        P("seq", None),
    )
    return jax.shard_map(
        local, mesh=mesh, in_specs=placed, out_specs=P("seq", "ch"), check_vma=False
    )
```
